32 devices in a mesh: groups: 2 (over x), blk: 16 (over z, y, core).
Axes of the slice: x: 2, y: 2, z: 4, core: 2. Of those that a mesh axis runs over, the one named last changes fastest.
Arguments:
- train_in: bfloat16 [32, 4096], P(('groups', 'blk')), parts along dimension 0, may hold values from -0.09375 to 0.09375
- train_out: bfloat16 [32, 14336], P(('groups', 'blk')), parts along dimension 0, may hold values from -0.050048828 to 0.050048828
- query_in: bfloat16 [64, 4096], P('groups'), parts along dimension 0, may hold values from -6 to 6
- query_out: bfloat16 [64, 14336], P('groups'), parts along dimension 0, may hold values from -6 to 6
- basis_in: bfloat16 [8192, 4096], P(('groups', 'blk')), parts along dimension 0, may hold values from -0.09375 to 0.09375
- basis_out: bfloat16 [28672, 14336], P(('groups', 'blk')), parts along dimension 0, may hold values from -0.046875 to 0.046875
- eigvals: float32 [28672, 4096], P(('groups', 'blk')), parts along dimension 0, may hold values from 0.05 to 18, as said below
Outputs:
- scores: float32 [32, 32], P(('groups', 'blk')), parts along dimension 0
The draws below stay inside these ranges and needn't reach their ends.
There are 2 independent parts, one for each index of `groups`. The reference program is written for one: setup_inputs(seed, part) draws one part's arguments, and reference() takes and returns one part's arrays. A program takes and returns all parts, laid end to end along the dimension named above; each array names one. Nothing has to cross between parts.
Inputs may be any that keep to these rules, and one draw needn't show every extreme that they name: `eigvals`: eigenvalue corrections, all positive.
All inputs are finite; a program needn't handle non-finite values.
Results may differ from the reference program's by a relative error of at most 0.006.
Values may be sent and summed in bfloat16 or wider, within the bound.
No kernel may reach another device: no remote copies, remote signals or barrier semaphores. Data moves between devices by JAX's collectives and lax.ppermute only.
A program may use at most 128 MiB of HBM per device.

```python
import math
import jax
import jax.numpy as jnp
from jax import lax

D_IN = 4096
D_OUT = 14336
NQ = 32
NTRAIN = 16


def draw_eigvals(key, part):
    key = jax.random.fold_in(key, 11)
    base = jnp.exp(jax.random.uniform(key, (D_OUT, D_IN), jnp.float32, math.log(0.05), math.log(2.0)))
    rising = 1.0 + 2.0 * jnp.arange(D_OUT, dtype=jnp.float32)[:, None] / D_OUT
    return base * rising


def block_scale(stream_key, dims, split, low, top_value):
    def one(dim, parts):
        draws = jax.random.uniform(jax.random.fold_in(jax.random.fold_in(stream_key, 6), dim), (parts,), jnp.float32, low / len(split), top_value / len(split))
        return jnp.repeat(jnp.exp(draws), dims[dim] // parts).reshape((-1,) + (1,) * (len(dims) - dim - 1))

    factor_of = one(*split[0])
    for cut in split[1:]:
        factor_of = factor_of * one(*cut)
    return factor_of


def centred(own_key, dims, deviation, bound, cuts=(), kind=jnp.bfloat16):
    array = jax.random.normal(own_key, dims, jnp.float32) * deviation
    if len(cuts) > 0:
        array = block_scale(own_key, dims, cuts, -0.22, 0.18) * array
    return jnp.clip(array, min=-bound, max=bound).astype(kind)


def setup_inputs(seed: int = 0, part: int = 0) -> dict:
    key_list = jax.random.split(jax.random.key(seed), 8)
    own_keys = jax.random.split(jax.random.fold_in(key_list[7], part), 8)
    return {
        "train_in": centred(own_keys[0], (NTRAIN, D_IN), (D_IN ** -0.5), 0.09375, ((0, 16),)),
        "train_out": centred(own_keys[1], (NTRAIN, D_OUT), (D_OUT ** -0.5), 0.050048828, ((0, 16),)),
        "query_in": centred(own_keys[2], (NQ, D_IN), 1.0, 6.0),
        "query_out": centred(own_keys[3], (NQ, D_OUT), 1.0, 6.0),
        "basis_in": centred(own_keys[4], (D_IN, D_IN), D_IN ** -0.5, 0.09375, ((0, 16),)),
        "basis_out": centred(own_keys[5], (D_OUT, D_OUT), D_OUT ** -0.5, 0.046875, ((0, 16),)),
        "eigvals": draw_eigvals(jax.random.fold_in(jax.random.fold_in(key_list[7], part), 71), part),
    }


def reference(train_in, train_out, query_in, query_out, basis_in, basis_out, eigvals):
    damping = 0.1 * jnp.sum(eigvals) / (D_OUT * D_IN)
    inverse = (1.0 / (eigvals + damping)).astype(jnp.bfloat16)
    stacked = jnp.concatenate([train_in, query_in], axis=0)
    contract = (((1,), (1,)), ((), ()))
    rot_in = lax.dot_general(stacked, basis_in, contract, preferred_element_type=jnp.float32).astype(jnp.bfloat16)
    count_train = train_in.shape[0]
    rot_train_in = rot_in[:count_train]
    rot_query_in = rot_in[count_train:]
    rot_train_out = lax.dot_general(train_out, basis_out, contract, preferred_element_type=jnp.float32).astype(jnp.bfloat16)
    rot_query_out = lax.dot_general(query_out, basis_out, contract, preferred_element_type=jnp.float32).astype(jnp.bfloat16)

    def one_query(operands):
        query_row, query_weight = operands
        pair = (rot_train_in.astype(jnp.float32) * query_row.astype(jnp.float32)[None, :]).astype(jnp.bfloat16)
        damped = lax.dot_general(pair, inverse, contract, preferred_element_type=jnp.float32)
        weight = rot_train_out.astype(jnp.float32) * query_weight.astype(jnp.float32)[None, :]
        return jnp.sum(damped * weight, axis=1)

    per_query = lax.map(one_query, (rot_query_in, rot_query_out))
    return jnp.transpose(per_query)
```

```python
import jax
import jax.numpy as jnp
from jax import lax
from jax.sharding import PartitionSpec as P

CONTRACT = (((1,), (1,)), ((), ()))


def stage_bits(count):
    bits = [1 << k for k in range(count.bit_length() - 1)]
    return bits[1:] + bits[:1]


def swap(piece, bit, count):
    return lax.ppermute(piece, "blk", [(i, i ^ bit) for i in range(count)])


def slot_order(count):
    order = [0]
    for bit in stage_bits(count):
        order = order + [j ^ bit for j in order]
    return order


def gather_slots(piece, count):
    for bit in stage_bits(count):
        piece = jnp.concatenate([piece, swap(piece, bit, count)], axis=0)
    return piece


def scatter_slots(piece, count):
    for bit in reversed(stage_bits(count)):
        half = piece.shape[0] // 2
        piece = piece[:half] + swap(piece[half:], bit, count)
    return piece


def dot(left, right):
    return lax.dot_general(left, right, CONTRACT, preferred_element_type=jnp.float32)


def split_sum(total):
    high = lax.reduce_precision(total, 8, 7)
    middle = lax.reduce_precision(total - high, 8, 7)
    low = total - high - middle
    return jnp.stack([high, middle, low]).astype(jnp.bfloat16)


def make_shards(count, d_in, d_out):
    def shards(train_in, train_out, query_in, query_out, basis_in, basis_out, eigvals):
        me = lax.axis_index("blk")
        order = jnp.asarray(slot_order(count), jnp.int32)
        local_train = train_in.shape[0]
        queries = query_in.shape[0]
        width = basis_in.shape[0]
        n_train = local_train * count

        sums = jnp.broadcast_to(split_sum(jnp.sum(eigvals))[:, None], (3, width))
        query_part = dot(query_in, basis_in).astype(jnp.bfloat16)
        out_query = dot(query_out, basis_out).astype(jnp.bfloat16)
        all_in = gather_slots(train_in, count)
        train_part = dot(all_in, basis_in).astype(jnp.bfloat16)
        train_part = train_part.reshape(count, local_train, width)
        train_part = jnp.take(train_part, jnp.argsort(order)[me ^ jnp.arange(count)], axis=0).reshape(n_train, width)
        parts = jnp.concatenate([train_part, query_part, sums], axis=0)
        gathered = gather_slots(parts[None], count)
        gathered = jnp.take(gathered, jnp.argsort(order)[me ^ jnp.arange(count)], axis=0)
        total = jnp.sum(gathered[:, n_train + queries :, 0].astype(jnp.float32))
        rotated = jnp.transpose(gathered[:, : n_train + queries], (1, 0, 2)).reshape(n_train + queries, -1)
        damping = 0.1 * total / (d_out * d_in)
        inverse = (1.0 / (eigvals + damping)).astype(jnp.bfloat16)

        all_out = gather_slots(train_out, count).reshape(count, local_train, -1)
        out_train = dot(all_out.reshape(n_train, -1), basis_out).astype(jnp.bfloat16)

        in_train = rotated[:n_train].reshape(count, local_train, -1)
        in_train = jnp.take(in_train, me ^ order, axis=0).reshape(n_train, -1)
        in_query = rotated[n_train:]
        pair = in_train[:, None, :] * in_query[None, :, :]
        damped = dot(pair.reshape(n_train * queries, -1), inverse).reshape(n_train, queries, -1)
        weight = out_train.astype(jnp.float32)[:, None, :] * out_query.astype(jnp.float32)[None, :, :]
        terms = jnp.sum(damped * weight, axis=2)
        return scatter_slots(terms, count)

    return shards


def solution(mesh):
    in_specs = (
        P(("groups", "blk"), None),
        P(("groups", "blk"), None),
        P("groups", None),
        P("groups", None),
        P(("groups", "blk"), None),
        P(("groups", "blk"), None),
        P(("groups", "blk"), None),
    )
    out_specs = P(("groups", "blk"), None)
    count = mesh.shape["blk"]

    def run(train_in, train_out, query_in, query_out, basis_in, basis_out, eigvals):
        shards = make_shards(count, train_in.shape[1], train_out.shape[1])
        return jax.shard_map(shards, mesh=mesh, in_specs=in_specs, out_specs=out_specs, check_vma=False)(
            train_in, train_out, query_in, query_out, basis_in, basis_out, eigvals
        )

    return run
```

```python
import jax
import jax.numpy as jnp
from jax import lax
from jax.experimental import pallas as pl
from jax.experimental.pallas import tpu as pltpu
from jax.sharding import PartitionSpec as P

CONTRACT = (((1,), (1,)), ((), ()))
SUM_ROWS = 8
BF16, F32 = jnp.bfloat16, jnp.float32
VMEM, SMEM = pltpu.VMEM, pltpu.SMEM


def stage_bits(count):
    return [1 << k for k in range(count.bit_length() - 1)][::-1]


def swap(piece, bit, count):
    return lax.ppermute(piece, "blk", [(i, i ^ bit) for i in range(count)])


def slot_order(count):
    order = [0]
    for bit in stage_bits(count):
        order = order + [j ^ bit for j in order]
    return order


def gather_slots(piece, count):
    for bit in stage_bits(count):
        piece = jnp.concatenate([piece, swap(piece, bit, count)], axis=0)
    return piece


def scatter_slots(piece, count):
    for bit in reversed(stage_bits(count)):
        half = piece.shape[0] // 2
        piece = piece[:half] + swap(piece[half:], bit, count)
    return piece


def dot(left, right):
    return lax.dot_general(left, right, CONTRACT, preferred_element_type=F32)


def slot_of(position, count):
    bits = count.bit_length() - 1
    out = jnp.zeros_like(position)
    for k in range(bits):
        out = out | (((position >> k) & 1) << (bits - 1 - k))
    return out


def row_permutation(me, count, local, transposed):
    n = count * local
    a = lax.broadcasted_iota(jnp.int32, (n, n), 0)
    b = lax.broadcasted_iota(jnp.int32, (n, n), 1)
    device, slot = (b, a) if transposed else (a, b)
    same = (device // local == (slot_of(slot // local, count) ^ me)) & (device % local == slot % local)
    return same.astype(F32).astype(BF16)


def whole(space=VMEM):
    return pl.BlockSpec(memory_space=space)


def sum_kernel(after_ref, before_ref, eig_ref, out_ref):
    @pl.when(pl.program_id(0) == 0)
    def _():
        out_ref[...] = before_ref[...]

    rows, columns = eig_ref.shape
    acc = eig_ref[:8, :]
    for i in range(1, rows // 8):
        acc = acc + eig_ref[i * 8 : (i + 1) * 8, :]
    part = acc[:, :128]
    for i in range(1, columns // 128):
        part = part + acc[:, i * 128 : (i + 1) * 128]
    out_ref[...] += part


def query_kernel(after_ref, query_ref, basis_ref, out_ref):
    out_ref[...] = dot(query_ref[...], basis_ref[...]).astype(BF16)


def train_kernel(count, local, d_in, me_ref, near_ref, far_ref, basis_ref, query_ref, sum_ref, out_ref):
    n_train = count * local
    queries = query_ref.shape[0]
    rows = jnp.concatenate([near_ref[:, :d_in], far_ref[:, :d_in]], axis=0)
    rotated = dot(rows, basis_ref[...]).astype(BF16)
    order = row_permutation(me_ref[0], count, local, False)
    out_ref[:n_train, :] = jnp.dot(order, rotated, preferred_element_type=F32).astype(BF16)
    out_ref[n_train : n_train + queries, :] = query_ref[...]
    whole_sum = jnp.full((SUM_ROWS, out_ref.shape[1]), jnp.sum(sum_ref[...]), F32)
    high = whole_sum.astype(BF16).astype(F32)
    middle = (whole_sum - high).astype(BF16).astype(F32)
    low = whole_sum - high - middle
    row = lax.broadcasted_iota(jnp.int32, whole_sum.shape, 0)
    pieces = jnp.where(row == 0, high, jnp.where(row == 1, middle, jnp.where(row == 2, low, 0.0)))
    out_ref[n_train + queries :, :] = pieces.astype(BF16)


def stack_kernel(d_in, near_ref, far_ref, query_ref, out_ref):
    half = near_ref.shape[0]
    out_ref[: 2 * half, :] = jnp.concatenate([near_ref[:, d_in:], far_ref[:, d_in:]], axis=0)
    out_ref[2 * half :, :] = query_ref[...]


def out_kernel(after_ref, before_ref, stacked_ref, basis_ref, out_ref):
    @pl.when(pl.program_id(0) == 0)
    def _():
        out_ref[...] = before_ref[...]

    out_ref[...] += dot(basis_ref[...], stacked_ref[...])


def first_out_kernel(after_ref, stacked_ref, basis_ref, out_ref):
    part = dot(basis_ref[...], stacked_ref[...])

    @pl.when(pl.program_id(0) == 0)
    def _():
        out_ref[...] = part

    @pl.when(pl.program_id(0) > 0)
    def _():
        out_ref[...] += part


def pack_kernel(d_in, in_ref, out_ref, held_ref):
    held_ref[:, :d_in] = in_ref[...]
    held_ref[:, d_in:] = out_ref[...]


def join_kernel(after_ref, near_ref, far_ref, out_ref):
    half = near_ref.shape[0]
    out_ref[:half] = near_ref[...]
    out_ref[half:] = far_ref[...]


def main_kernel(count, local, queries, scale, chunks, deep, *refs):
    me_ref, sums_near, sums_far, near_ref, far_ref, eig_ref, out_ref, terms_ref, acc, eig, sems = refs
    me = me_ref[0]
    n_train = count * local
    half, _, width = near_ref.shape
    copies = []
    for j, slot in enumerate(chunks):
        column = j * width if slot is None else pl.multiple_of((me ^ slot) * width, width)
        copies.append(pltpu.make_async_copy(eig_ref.at[:, pl.ds(column, width)], eig.at[j], sems.at[j]))
    for copy in copies[:deep]:
        copy.start()
    first = n_train + queries
    total = jnp.sum(sums_near[:, first:, :].astype(F32)) + jnp.sum(sums_far[:, first:, :].astype(F32))
    damping = total / sums_near.shape[2] * scale
    order = row_permutation(me, count, local, True)

    def operands(j):
        copies[j].wait()
        if j + deep < len(chunks):
            copies[j + deep].start()
        inverse = (1.0 / (eig[j] + damping)).astype(BF16)
        block = near_ref.at[j] if j < half else far_ref.at[j - half]
        rows = jnp.dot(order, block[:n_train, :], preferred_element_type=F32).astype(BF16)
        pair = rows[:, None, :] * block[n_train:first, :][None, :, :]
        return inverse, pair.reshape(n_train * queries, width)

    ready = operands(0)
    for j in range(len(chunks)):
        inverse, pair = ready
        if j + 1 < len(chunks):
            ready = operands(j + 1)
        part = dot(inverse, pair)
        if j == 0:
            acc[...] = part
        else:
            acc[...] += part
    pairs = n_train * queries
    column = lax.broadcasted_iota(jnp.int32, (n_train, pairs), 1)
    row = lax.broadcasted_iota(jnp.int32, (n_train, pairs), 0)
    spread_train = (column // queries == row).astype(F32).astype(BF16)
    column = lax.broadcasted_iota(jnp.int32, (queries, pairs), 1)
    row = lax.broadcasted_iota(jnp.int32, (queries, pairs), 0)
    spread_query = (column % queries == row).astype(F32).astype(BF16)
    out = out_ref[...].astype(BF16)
    weight = jnp.dot(out[:, :n_train], spread_train, preferred_element_type=F32)
    weight = weight * jnp.dot(out[:, n_train:], spread_query, preferred_element_type=F32)
    terms_ref[...] = jnp.sum(acc[...] * weight, axis=0, keepdims=True)


def make_shards(count, d_in, d_out):
    def shards(train_in, train_out, query_in, query_out, basis_in, basis_out, eigvals):
        me = lax.axis_index("blk").astype(jnp.int32).reshape(1)
        local = train_in.shape[0]
        queries = query_in.shape[0]
        width = basis_in.shape[0]
        rows = basis_out.shape[0]
        n_train = local * count
        bits = stage_bits(count)
        pieces = 4 if rows % 64 == 0 else 1
        piece = rows // pieces
        steps = 2 if piece % 32 == 0 else 1
        block = piece // steps
        params = pltpu.CompilerParams(vmem_limit_bytes=32 * 2**20)
        eig_far = pltpu.with_memory_space_constraint(eigvals, pltpu.HBM)
        basis_far = pltpu.with_memory_space_constraint(basis_out, pltpu.HBM)

        def eig_sum(index, after, before):
            return pl.pallas_call(
                sum_kernel,
                grid=(steps,),
                out_shape=jax.ShapeDtypeStruct((8, 128), F32),
                in_specs=[
                    whole(pl.ANY),
                    pl.BlockSpec((8, 128), lambda i: (0, 0)),
                    pl.BlockSpec((block, d_in), lambda i: (index * steps + i, 0)),
                ],
                out_specs=pl.BlockSpec((8, 128), lambda i: (0, 0)),
                compiler_params=params,
                cost_estimate=pl.CostEstimate(flops=piece * d_in, bytes_accessed=4 * piece * d_in, transcendentals=0),
                name="eig_sum",
            )(after, before, eig_far)

        stretch = 896 if d_out % (len(bits) * 896) == 0 else d_out // len(bits)
        stretches = d_out // len(bits) // stretch if len(bits) == 4 else d_out // stretch

        def rotate_out(index, after, before, stacked):
            shape = (rows, n_train + queries)
            out = pl.BlockSpec(shape, lambda i: (0, 0))
            places = [
                pl.BlockSpec((shape[1], stretch), lambda i: (0, index * stretches + i)),
                pl.BlockSpec((rows, stretch), lambda i: (0, index * stretches + i)),
            ]
            return pl.pallas_call(
                first_out_kernel if before is None else out_kernel,
                grid=(stretches,),
                out_shape=jax.ShapeDtypeStruct(shape, F32),
                in_specs=[whole(pl.ANY)] + ([] if before is None else [out]) + places,
                out_specs=out,
                compiler_params=params,
                cost_estimate=pl.CostEstimate(
                    flops=2 * rows * stretch * stretches * shape[1],
                    bytes_accessed=2 * rows * stretch * stretches,
                    transcendentals=0,
                ),
                name="rotate_out",
            )(after, *([] if before is None else [before]), stacked, basis_far)

        def join(after, near, far):
            return pl.pallas_call(
                join_kernel,
                out_shape=jax.ShapeDtypeStruct((2 * near.shape[0],) + near.shape[1:], near.dtype),
                in_specs=[whole(pl.ANY), whole(), whole()],
                out_specs=whole(),
                compiler_params=params,
                name="join",
            )(after, near, far)

        held = pl.pallas_call(
            lambda in_ref, out_ref, held_ref: pack_kernel(d_in, in_ref, out_ref, held_ref),
            out_shape=jax.ShapeDtypeStruct((local, d_in + d_out), BF16),
            in_specs=[whole()] * 2,
            out_specs=whole(),
            compiler_params=params,
            name="pack",
        )(train_in, train_out)
        total = jnp.zeros((8, 128), F32)
        query_part = None
        after = me
        for k, bit in enumerate(bits):
            got = swap(held, bit, count)
            if k == min(1, len(bits) - 1):
                query_part = pl.pallas_call(
                    query_kernel,
                    out_shape=jax.ShapeDtypeStruct((queries, width), BF16),
                    in_specs=[whole(pl.ANY), whole(), whole()],
                    out_specs=whole(),
                    compiler_params=params,
                    name="query_in",
                )(after, query_in, basis_in)
            if k < pieces:
                total = eig_sum(k, after, total)
            after = got
            if k < len(bits) - 1:
                held = join(total, held, got)
        near, far = held, got
        parts = pl.pallas_call(
            lambda *refs: train_kernel(count, local, d_in, *refs),
            out_shape=jax.ShapeDtypeStruct((n_train + queries + SUM_ROWS, width), BF16),
            in_specs=[whole(SMEM)] + [whole()] * 5,
            out_specs=whole(),
            compiler_params=params,
            name="train_in",
        )(me, near, far, basis_in, query_part, total)
        stacked = pl.pallas_call(
            lambda *refs: stack_kernel(d_in, *refs),
            out_shape=jax.ShapeDtypeStruct((n_train + queries, d_out), BF16),
            in_specs=[whole()] * 3,
            out_specs=whole(),
            compiler_params=params,
            name="stack",
        )(near, far, query_out)
        held = parts[None]
        after = parts
        out_part = None
        for k, bit in enumerate(bits):
            got = swap(held, bit, count)
            if (k + 1) * stretch * stretches <= d_out:
                out_part = rotate_out(k, after, out_part, stacked)
            after = got
            if k < len(bits) - 1:
                held = join(out_part, held, got)
        near, far = held, got
        sums = (near, far)
        order = slot_order(count)
        if width % 128 == 0:
            chunks = order
        else:
            chunk = 256
            chunks = [None] * (d_in // chunk)
            back = jnp.argsort(jnp.asarray(order, jnp.int32))[me[0] ^ jnp.arange(count)]
            flat = jnp.take(jnp.concatenate([near, far], axis=0), back, axis=0).transpose(1, 0, 2)
            flat = flat.reshape(flat.shape[0], len(chunks), chunk).transpose(1, 0, 2)
            near, far = flat[: len(chunks) // 2], flat[len(chunks) // 2 :]
        terms = pl.pallas_call(
            lambda *refs: main_kernel(count, local, queries, 0.1 / (d_out * d_in), chunks, 4, *refs),
            out_shape=jax.ShapeDtypeStruct((1, n_train * queries), F32),
            in_specs=[whole(SMEM)] + [whole()] * 4 + [whole(pltpu.HBM), whole()],
            out_specs=whole(),
            scratch_shapes=[
                pltpu.VMEM((rows, n_train * queries), F32),
                pltpu.VMEM((len(chunks), rows, near.shape[2]), F32),
                pltpu.SemaphoreType.DMA((len(chunks),)),
            ],
            compiler_params=params,
            name="scores",
        )(me, *sums, near, far, eig_far, out_part)
        return scatter_slots(terms.reshape(n_train, queries), count)

    return shards


def solution(mesh):
    in_specs = (
        P(("groups", "blk"), None),
        P(("groups", "blk"), None),
        P("groups", None),
        P("groups", None),
        P(("groups", "blk"), None),
        P(("groups", "blk"), None),
        P(("groups", "blk"), None),
    )
    out_specs = P(("groups", "blk"), None)
    count = mesh.shape["blk"]

    def run(train_in, train_out, query_in, query_out, basis_in, basis_out, eigvals):
        shards = make_shards(count, train_in.shape[1], train_out.shape[1])
        return jax.shard_map(shards, mesh=mesh, in_specs=in_specs, out_specs=out_specs, check_vma=False)(
            train_in, train_out, query_in, query_out, basis_in, basis_out, eigvals
        )

    return run
```

```python
import jax
import jax.numpy as jnp
from jax import lax
from jax.experimental import pallas as pl
from jax.experimental.pallas import tpu as pltpu
from jax.sharding import PartitionSpec as P

CONTRACT = (((1,), (1,)), ((), ()))
SUM_ROWS = 8
class Fixed(int):
    pass


BF16, F32 = jnp.bfloat16, jnp.float32
VMEM, SMEM = pltpu.VMEM, pltpu.SMEM


def stage_bits(count):
    return [1 << k for k in range(count.bit_length() - 1)][::-1]


def swap(piece, bit, count):
    return lax.ppermute(piece, "blk", [(i, i ^ bit) for i in range(count)])


def slot_order(count):
    order = [0]
    for bit in stage_bits(count):
        order = order + [j ^ bit for j in order]
    return order


def gather_slots(piece, count):
    for bit in stage_bits(count):
        piece = jnp.concatenate([piece, swap(piece, bit, count)], axis=0)
    return piece


def scatter_slots(piece, count):
    for bit in reversed(stage_bits(count)):
        half = piece.shape[0] // 2
        piece = piece[:half] + swap(piece[half:], bit, count)
    return piece


def dot(left, right):
    return lax.dot_general(left, right, CONTRACT, preferred_element_type=F32)


def slot_of(position, count):
    bits = count.bit_length() - 1
    out = jnp.zeros_like(position)
    for k in range(bits):
        out = out | (((position >> k) & 1) << (bits - 1 - k))
    return out


def row_permutation(me, count, local, transposed):
    n = count * local
    a = lax.broadcasted_iota(jnp.int32, (n, n), 0)
    b = lax.broadcasted_iota(jnp.int32, (n, n), 1)
    device, slot = (b, a) if transposed else (a, b)
    same = (device // local == (slot_of(slot // local, count) ^ me)) & (device % local == slot % local)
    return same.astype(F32).astype(BF16)


def whole(space=VMEM):
    return pl.BlockSpec(memory_space=space)


def sum_kernel(after_ref, before_ref, eig_ref, out_ref):
    @pl.when(pl.program_id(0) == 0)
    def _():
        out_ref[...] = before_ref[...]

    rows, columns = eig_ref.shape
    acc = eig_ref[:8, :]
    for i in range(1, rows // 8):
        acc = acc + eig_ref[i * 8 : (i + 1) * 8, :]
    part = acc[:, :128]
    for i in range(1, columns // 128):
        part = part + acc[:, i * 128 : (i + 1) * 128]
    out_ref[...] += part


def query_kernel(after_ref, query_ref, basis_ref, out_ref):
    out_ref[...] = dot(query_ref[...], basis_ref[...]).astype(BF16)


def train_kernel(count, local, d_in, me_ref, near_ref, far_ref, basis_ref, query_ref, sum_ref, out_ref):
    n_train = count * local
    queries = query_ref.shape[0]
    rows = jnp.concatenate([near_ref[:, :d_in], far_ref[:, :d_in]], axis=0)
    rotated = dot(rows, basis_ref[...]).astype(BF16)
    order = row_permutation(me_ref[0], count, local, False)
    out_ref[:n_train, :] = jnp.dot(order, rotated, preferred_element_type=F32).astype(BF16)
    out_ref[n_train : n_train + queries, :] = query_ref[...]
    whole_sum = jnp.full((SUM_ROWS, out_ref.shape[1]), jnp.sum(sum_ref[...]), F32)
    high = whole_sum.astype(BF16).astype(F32)
    middle = (whole_sum - high).astype(BF16).astype(F32)
    low = whole_sum - high - middle
    row = lax.broadcasted_iota(jnp.int32, whole_sum.shape, 0)
    pieces = jnp.where(row == 0, high, jnp.where(row == 1, middle, jnp.where(row == 2, low, 0.0)))
    out_ref[n_train + queries :, :] = pieces.astype(BF16)


def stack_kernel(d_in, near_ref, far_ref, query_ref, out_ref):
    half = near_ref.shape[0]
    out_ref[: 2 * half, :] = jnp.concatenate([near_ref[:, d_in:], far_ref[:, d_in:]], axis=0)
    out_ref[2 * half :, :] = query_ref[...]


def fetch(basis_ref, begin, width, held_ref, sems):
    rows = held_ref.shape[0]
    parts = sems.shape[0]
    copies = []
    for c in range(parts):
        place = pl.ds(c * (rows // parts), rows // parts)
        copies.append(pltpu.make_async_copy(basis_ref.at[place, pl.ds(begin, width)], held_ref.at[place], sems.at[c]))
    for copy in copies:
        copy.start()
    return copies


def load_kernel(begin, after_ref, basis_ref, next_ref, sems):
    for copy in fetch(basis_ref, begin, next_ref.shape[1], next_ref, sems):
        copy.wait()


def out_kernel(begin, after_ref, before_ref, stacked_ref, held_ref, basis_ref, out_ref, next_ref, sems):
    width = held_ref.shape[1]
    copies = fetch(basis_ref, begin + width, next_ref.shape[1], next_ref, sems)
    out_ref[...] = before_ref[...] + dot(held_ref[...], stacked_ref[:, pl.ds(begin, width)])
    for copy in copies:
        copy.wait()


def last_out_kernel(begin, chunks, me_ref, after_ref, before_ref, stacked_ref, held_ref, eig_ref, out_ref, early_ref, sems):
    width = held_ref.shape[1]
    copies = eig_copies(me_ref[0], chunks, eig_ref, early_ref, sems)
    for copy in copies:
        copy.start()
    out_ref[...] = before_ref[...] + dot(held_ref[...], stacked_ref[:, pl.ds(begin, width)])
    for copy in copies:
        copy.wait()


def eig_copies(me, chunks, eig_ref, eig, sems):
    width = eig.shape[2]
    copies = []
    for j, slot in enumerate(chunks):
        column = slot * width if isinstance(slot, Fixed) else pl.multiple_of((me ^ slot) * width, width)
        copies.append(pltpu.make_async_copy(eig_ref.at[:, pl.ds(column, width)], eig.at[j], sems.at[j]))
    return copies


def pack_kernel(d_in, in_ref, out_ref, held_ref, sems):
    first = pltpu.make_async_copy(in_ref, held_ref.at[:, :d_in], sems.at[0])
    second = pltpu.make_async_copy(out_ref, held_ref.at[:, d_in:], sems.at[1])
    first.start()
    second.start()
    first.wait()
    second.wait()


def join_kernel(after_ref, other_ref, near_ref, far_ref, out_ref):
    half = near_ref.shape[0]
    out_ref[:half] = near_ref[...]
    out_ref[half:] = far_ref[...]


def main_kernel(count, local, queries, scale, chunks, deep, *refs):
    me_ref, sums_near, sums_far, near_ref, far_ref, eig_ref, early_ref, out_ref, terms_ref, acc, eig, sems = refs
    me = me_ref[0]
    n_train = count * local
    half, _, width = near_ref.shape
    early = early_ref.shape[0]
    copies = eig_copies(me, chunks[early:], eig_ref, eig, sems)
    for copy in copies[:deep]:
        copy.start()
    first = n_train + queries
    total = jnp.sum(sums_near[:, first:, :].astype(F32)) + jnp.sum(sums_far[:, first:, :].astype(F32))
    damping = total / sums_near.shape[2] * scale
    order = row_permutation(me, count, local, True)

    def operands(j):
        if j >= early:
            copies[j - early].wait()
            if j - early + deep < len(copies):
                copies[j - early + deep].start()
        values = early_ref[j] if j < early else eig[j - early]
        inverse = (1.0 / (values + damping)).astype(BF16)
        block = near_ref.at[j] if j < half else far_ref.at[j - half]
        rows = jnp.dot(order, block[:n_train, :], preferred_element_type=F32).astype(BF16)
        pair = rows[:, None, :] * block[n_train:first, :][None, :, :]
        return inverse, pair.reshape(n_train * queries, width)

    ready = operands(0)
    for j in range(len(chunks)):
        inverse, pair = ready
        if j + 1 < len(chunks):
            ready = operands(j + 1)
        part = dot(inverse, pair)
        if j == 0:
            acc[...] = part
        else:
            acc[...] += part
    pairs = n_train * queries
    column = lax.broadcasted_iota(jnp.int32, (n_train, pairs), 1)
    row = lax.broadcasted_iota(jnp.int32, (n_train, pairs), 0)
    spread_train = (column // queries == row).astype(F32).astype(BF16)
    column = lax.broadcasted_iota(jnp.int32, (queries, pairs), 1)
    row = lax.broadcasted_iota(jnp.int32, (queries, pairs), 0)
    spread_query = (column % queries == row).astype(F32).astype(BF16)
    out = out_ref[...].astype(BF16)
    weight = jnp.dot(out[:, :n_train], spread_train, preferred_element_type=F32)
    weight = weight * jnp.dot(out[:, n_train:], spread_query, preferred_element_type=F32)
    terms_ref[...] = jnp.sum(acc[...] * weight, axis=0, keepdims=True)


def make_shards(count, d_in, d_out):
    def shards(train_in, train_out, query_in, query_out, basis_in, basis_out, eigvals):
        me = lax.axis_index("blk").astype(jnp.int32).reshape(1)
        local = train_in.shape[0]
        queries = query_in.shape[0]
        width = basis_in.shape[0]
        rows = basis_out.shape[0]
        n_train = local * count
        bits = stage_bits(count)
        order = slot_order(count)
        chunk = width if width % 128 == 0 else 256
        chunks = order if width % 128 == 0 else [Fixed(k) for k in range(d_in // chunk)]
        early = min(4, len(chunks) - 1)
        block = 112 if rows % 112 == 0 else rows
        blocks = rows // block
        pieces = max(1, len(bits) - 1)
        cuts = [-(-k * blocks // pieces) for k in range(pieces + 1)]
        params = pltpu.CompilerParams(vmem_limit_bytes=20 * 2**20)
        eig_far = pltpu.with_memory_space_constraint(eigvals, pltpu.HBM)
        basis_far = pltpu.with_memory_space_constraint(basis_out, pltpu.HBM)

        def eig_sum(index, after, before):
            return pl.pallas_call(
                sum_kernel,
                grid=(cuts[index + 1] - cuts[index],),
                out_shape=jax.ShapeDtypeStruct((8, 128), F32),
                in_specs=[
                    whole(pl.ANY),
                    pl.BlockSpec((8, 128), lambda i: (0, 0)),
                    pl.BlockSpec((block, d_in), lambda i: (cuts[index] + i, 0)),
                ],
                out_specs=pl.BlockSpec((8, 128), lambda i: (0, 0)),
                compiler_params=params,
                cost_estimate=pl.CostEstimate(flops=rows * d_in // 4, bytes_accessed=rows * d_in, transcendentals=0),
                name="eig_sum",
            )(after, before, eig_far)

        stretch = 128
        stretches = d_out // stretch
        turns = min(len(bits), 4)
        out_cuts = [k * stretches // turns * stretch for k in range(turns + 1)]
        parts = 4 if rows % 64 == 0 else 1

        def held_shape(index):
            return jax.ShapeDtypeStruct((rows, out_cuts[index + 1] - out_cuts[index]), BF16)

        def load_first(after):
            return pl.pallas_call(
                lambda *refs: load_kernel(0, *refs),
                out_shape=held_shape(0),
                in_specs=[whole(pl.ANY), whole(pltpu.HBM)],
                out_specs=whole(),
                scratch_shapes=[pltpu.SemaphoreType.DMA((parts,))],
                compiler_params=params,
                cost_estimate=pl.CostEstimate(flops=0, bytes_accessed=rows * d_out // 2, transcendentals=0),
                name="load",
            )(after, basis_far)

        def rotate_out(index, after, before, stacked, held):
            out = jax.ShapeDtypeStruct((rows, n_train + queries), F32)
            cost = pl.CostEstimate(
                flops=rows * d_out * (n_train + queries) // 2, bytes_accessed=rows * d_out // 2, transcendentals=0
            )
            if index + 1 < turns:
                return pl.pallas_call(
                    lambda *refs: out_kernel(out_cuts[index], *refs),
                    out_shape=(out, held_shape(index + 1)),
                    in_specs=[whole(pl.ANY)] + [whole()] * 3 + [whole(pltpu.HBM)],
                    out_specs=(whole(), whole()),
                    scratch_shapes=[pltpu.SemaphoreType.DMA((parts,))],
                    compiler_params=params,
                    cost_estimate=cost,
                    name="rotate_out",
                )(after, before, stacked, held, basis_far)
            return pl.pallas_call(
                lambda *refs: last_out_kernel(out_cuts[index], chunks[:early], *refs),
                out_shape=(out, jax.ShapeDtypeStruct((early, rows, chunk), F32)),
                in_specs=[whole(SMEM), whole(pl.ANY)] + [whole()] * 3 + [whole(pltpu.HBM)],
                out_specs=(whole(), whole()),
                scratch_shapes=[pltpu.SemaphoreType.DMA((early,))],
                compiler_params=params,
                cost_estimate=cost,
                name="rotate_out_last",
            )(me, after, before, stacked, held, eig_far)

        def join(after, near, far, other=None):
            return pl.pallas_call(
                join_kernel,
                out_shape=jax.ShapeDtypeStruct((2 * near.shape[0],) + near.shape[1:], near.dtype),
                in_specs=[whole(pl.ANY), whole(pl.ANY), whole(), whole()],
                out_specs=whole(),
                compiler_params=params,
                name="join",
            )(after, after if other is None else other, near, far)

        held = pl.pallas_call(
            lambda *refs: pack_kernel(d_in, *refs),
            out_shape=jax.ShapeDtypeStruct((local, d_in + d_out), BF16),
            in_specs=[whole(pltpu.HBM)] * 2,
            out_specs=whole(),
            scratch_shapes=[pltpu.SemaphoreType.DMA((2,))],
            compiler_params=params,
            name="pack",
        )(pltpu.with_memory_space_constraint(train_in, pltpu.HBM), pltpu.with_memory_space_constraint(train_out, pltpu.HBM))
        total = jnp.zeros((8, 128), F32)
        query_part = None
        after = me
        for k, bit in enumerate(bits):
            got = swap(held, bit, count)
            if k == min(2, len(bits) - 1):
                query_part = pl.pallas_call(
                    query_kernel,
                    out_shape=jax.ShapeDtypeStruct((queries, width), BF16),
                    in_specs=[whole(pl.ANY), whole(), whole()],
                    out_specs=whole(),
                    compiler_params=params,
                    name="query_in",
                )(after, query_in, basis_in)
            if k < pieces and cuts[k] < cuts[k + 1]:
                total = eig_sum(k, after, total)
            after = got
            if k < len(bits) - 1:
                held = join(total, held, got, query_part)
        near, far = held, got
        basis_held = load_first(held)
        merged = pl.pallas_call(
            lambda *refs: train_kernel(count, local, d_in, *refs),
            out_shape=jax.ShapeDtypeStruct((n_train + queries + SUM_ROWS, width), BF16),
            in_specs=[whole(SMEM)] + [whole()] * 5,
            out_specs=whole(),
            compiler_params=params,
            name="train_in",
        )(me, near, far, basis_in, query_part, total)
        stacked = pl.pallas_call(
            lambda *refs: stack_kernel(d_in, *refs),
            out_shape=jax.ShapeDtypeStruct((n_train + queries, d_out), BF16),
            in_specs=[whole()] * 3,
            out_specs=whole(),
            compiler_params=params,
            name="stack",
        )(near, far, query_out)
        held = merged[None]
        after = merged
        out_part = jnp.zeros((rows, n_train + queries), F32)
        for k, bit in enumerate(bits):
            got = swap(held, bit, count)
            if k < turns:
                out_part, basis_held = rotate_out(k, after, out_part, stacked, basis_held)
            after = got
            if k < len(bits) - 1:
                held = join(out_part, held, got)
        near, far = held, got
        sums = (near, far)
        if isinstance(chunks[0], Fixed):
            back = jnp.argsort(jnp.asarray(order, jnp.int32))[me[0] ^ jnp.arange(count)]
            flat = jnp.take(jnp.concatenate([near, far], axis=0), back, axis=0).transpose(1, 0, 2)
            flat = flat.reshape(flat.shape[0], len(chunks), chunk).transpose(1, 0, 2)
            near, far = flat[: len(chunks) // 2], flat[len(chunks) // 2 :]
        terms = pl.pallas_call(
            lambda *refs: main_kernel(count, local, queries, 0.1 / (d_out * d_in), chunks, 4, *refs),
            out_shape=jax.ShapeDtypeStruct((1, n_train * queries), F32),
            in_specs=[whole(SMEM)] + [whole()] * 4 + [whole(pltpu.HBM), whole(), whole()],
            out_specs=whole(),
            scratch_shapes=[
                pltpu.VMEM((rows, n_train * queries), F32),
                pltpu.VMEM((len(chunks) - early, rows, chunk), F32),
                pltpu.SemaphoreType.DMA((len(chunks) - early,)),
            ],
            compiler_params=params,
            name="scores",
        )(me, *sums, near, far, eig_far, basis_held, out_part)
        return scatter_slots(terms.reshape(n_train, queries), count)

    return shards


def solution(mesh):
    in_specs = (
        P(("groups", "blk"), None),
        P(("groups", "blk"), None),
        P("groups", None),
        P("groups", None),
        P(("groups", "blk"), None),
        P(("groups", "blk"), None),
        P(("groups", "blk"), None),
    )
    out_specs = P(("groups", "blk"), None)
    count = mesh.shape["blk"]

    def run(train_in, train_out, query_in, query_out, basis_in, basis_out, eigvals):
        shards = make_shards(count, train_in.shape[1], train_out.shape[1])
        return jax.shard_map(shards, mesh=mesh, in_specs=in_specs, out_specs=out_specs, check_vma=False)(
            train_in, train_out, query_in, query_out, basis_in, basis_out, eigvals
        )

    return run
```

```python
import jax
import jax.numpy as jnp
from jax import lax
from jax.experimental import pallas as pl
from jax.experimental.pallas import tpu as pltpu
from jax.sharding import PartitionSpec as P

CONTRACT = (((1,), (1,)), ((), ()))
SUM_ROWS = 8
class Fixed(int):
    pass


BF16, F32 = jnp.bfloat16, jnp.float32
VMEM, SMEM = pltpu.VMEM, pltpu.SMEM


def stage_bits(count):
    return [1 << k for k in range(count.bit_length() - 1)][::-1]


def swap(piece, bit, count):
    return lax.ppermute(piece, "blk", [(i, i ^ bit) for i in range(count)])


def slot_order(count):
    order = [0]
    for bit in stage_bits(count):
        order = order + [j ^ bit for j in order]
    return order


def gather_slots(piece, count):
    for bit in stage_bits(count):
        piece = jnp.concatenate([piece, swap(piece, bit, count)], axis=0)
    return piece


def scatter_slots(piece, count):
    for bit in reversed(stage_bits(count)):
        half = piece.shape[0] // 2
        piece = piece[:half] + swap(piece[half:], bit, count)
    return piece


def dot(left, right):
    return lax.dot_general(left, right, CONTRACT, preferred_element_type=F32)


def slot_of(position, count):
    bits = count.bit_length() - 1
    out = jnp.zeros_like(position)
    for k in range(bits):
        out = out | (((position >> k) & 1) << (bits - 1 - k))
    return out


def row_permutation(me, count, local, transposed):
    n = count * local
    a = lax.broadcasted_iota(jnp.int32, (n, n), 0)
    b = lax.broadcasted_iota(jnp.int32, (n, n), 1)
    device, slot = (b, a) if transposed else (a, b)
    same = (device // local == (slot_of(slot // local, count) ^ me)) & (device % local == slot % local)
    return same.astype(F32).astype(BF16)


def whole(space=VMEM):
    return pl.BlockSpec(memory_space=space)


def sum_kernel(after_ref, before_ref, eig_ref, out_ref):
    @pl.when(pl.program_id(0) == 0)
    def _():
        out_ref[...] = before_ref[...]

    rows, columns = eig_ref.shape
    acc = eig_ref[:8, :]
    for i in range(1, rows // 8):
        acc = acc + eig_ref[i * 8 : (i + 1) * 8, :]
    part = acc[:, :128]
    for i in range(1, columns // 128):
        part = part + acc[:, i * 128 : (i + 1) * 128]
    out_ref[...] += part


def query_kernel(after_ref, query_ref, basis_ref, out_ref):
    out_ref[...] = dot(query_ref[...], basis_ref[...]).astype(BF16)


def train_kernel(count, local, d_in, me_ref, near_ref, far_ref, basis_ref, query_ref, sum_ref, out_ref):
    n_train = count * local
    queries = query_ref.shape[0]
    rows = jnp.concatenate([near_ref[:, :d_in], far_ref[:, :d_in]], axis=0)
    rotated = dot(rows, basis_ref[...]).astype(BF16)
    order = row_permutation(me_ref[0], count, local, False)
    out_ref[:n_train, :] = jnp.dot(order, rotated, preferred_element_type=F32).astype(BF16)
    out_ref[n_train : n_train + queries, :] = query_ref[...]
    whole_sum = jnp.full((SUM_ROWS, out_ref.shape[1]), jnp.sum(sum_ref[...]), F32)
    high = whole_sum.astype(BF16).astype(F32)
    middle = (whole_sum - high).astype(BF16).astype(F32)
    low = whole_sum - high - middle
    row = lax.broadcasted_iota(jnp.int32, whole_sum.shape, 0)
    pieces = jnp.where(row == 0, high, jnp.where(row == 1, middle, jnp.where(row == 2, low, 0.0)))
    out_ref[n_train + queries :, :] = pieces.astype(BF16)


def stack_kernel(d_in, near_ref, far_ref, query_ref, out_ref):
    half = near_ref.shape[0]
    out_ref[: 2 * half, :] = jnp.concatenate([near_ref[:, d_in:], far_ref[:, d_in:]], axis=0)
    out_ref[2 * half :, :] = query_ref[...]


def fetch(basis_ref, begin, width, held_ref, sems):
    rows = held_ref.shape[0]
    parts = sems.shape[0]
    copies = []
    for c in range(parts):
        place = pl.ds(c * (rows // parts), rows // parts)
        copies.append(pltpu.make_async_copy(basis_ref.at[place, pl.ds(begin, width)], held_ref.at[place], sems.at[c]))
    for copy in copies:
        copy.start()
    return copies


def load_kernel(begin, after_ref, basis_ref, next_ref, sems):
    for copy in fetch(basis_ref, begin, next_ref.shape[1], next_ref, sems):
        copy.wait()


def out_kernel(begin, after_ref, before_ref, stacked_ref, held_ref, basis_ref, out_ref, next_ref, sems):
    width = held_ref.shape[1]
    copies = fetch(basis_ref, begin + width, next_ref.shape[1], next_ref, sems)
    out_ref[...] = before_ref[...] + dot(held_ref[...], stacked_ref[:, pl.ds(begin, width)])
    for copy in copies:
        copy.wait()


def last_out_kernel(begin, chunks, me_ref, after_ref, before_ref, stacked_ref, held_ref, eig_ref, out_ref, early_ref, sems):
    width = held_ref.shape[1]
    copies = eig_copies(me_ref[0], chunks, eig_ref, early_ref, sems)
    for copy in copies:
        copy.start()
    out_ref[...] = before_ref[...] + dot(held_ref[...], stacked_ref[:, pl.ds(begin, width)])
    for copy in copies:
        copy.wait()


def eig_copies(me, chunks, eig_ref, eig, sems):
    width = eig.shape[2]
    copies = []
    for j, slot in enumerate(chunks):
        column = slot * width if isinstance(slot, Fixed) else pl.multiple_of((me ^ slot) * width, width)
        copies.append(pltpu.make_async_copy(eig_ref.at[:, pl.ds(column, width)], eig.at[j], sems.at[j]))
    return copies


def pack_kernel(d_in, in_ref, out_ref, held_ref, sems):
    first = pltpu.make_async_copy(in_ref, held_ref.at[:, :d_in], sems.at[0])
    second = pltpu.make_async_copy(out_ref, held_ref.at[:, d_in:], sems.at[1])
    first.start()
    second.start()
    first.wait()
    second.wait()


def join_kernel(after_ref, other_ref, near_ref, far_ref, out_ref):
    half = near_ref.shape[0]
    out_ref[:half] = near_ref[...]
    out_ref[half:] = far_ref[...]


def main_kernel(count, local, queries, scale, chunks, deep, *refs):
    me_ref, sums_near, sums_far, near_ref, far_ref, eig_ref, early_ref, out_ref, terms_ref, acc, eig, sems = refs
    me = me_ref[0]
    n_train = count * local
    half, _, width = near_ref.shape
    early = early_ref.shape[0]
    copies = eig_copies(me, chunks[early:], eig_ref, eig, sems)
    for copy in copies[:deep]:
        copy.start()
    first = n_train + queries
    total = jnp.sum(sums_near[:, first:, :].astype(F32)) + jnp.sum(sums_far[:, first:, :].astype(F32))
    damping = total / sums_near.shape[2] * scale
    order = row_permutation(me, count, local, True)

    def operands(j):
        if j >= early:
            copies[j - early].wait()
            if j - early + deep < len(copies):
                copies[j - early + deep].start()
        values = early_ref[j] if j < early else eig[j - early]
        inverse = (1.0 / (values + damping)).astype(BF16)
        block = near_ref.at[j] if j < half else far_ref.at[j - half]
        rows = jnp.dot(order, block[:n_train, :], preferred_element_type=F32).astype(BF16)
        pair = rows[:, None, :] * block[n_train:first, :][None, :, :]
        return inverse, pair.reshape(n_train * queries, width)

    ready = operands(0)
    for j in range(len(chunks)):
        inverse, pair = ready
        if j + 1 < len(chunks):
            ready = operands(j + 1)
        part = dot(inverse, pair)
        if j == 0:
            acc[...] = part
        else:
            acc[...] += part
    pairs = n_train * queries
    column = lax.broadcasted_iota(jnp.int32, (n_train, pairs), 1)
    row = lax.broadcasted_iota(jnp.int32, (n_train, pairs), 0)
    spread_train = (column // queries == row).astype(F32).astype(BF16)
    column = lax.broadcasted_iota(jnp.int32, (queries, pairs), 1)
    row = lax.broadcasted_iota(jnp.int32, (queries, pairs), 0)
    spread_query = (column % queries == row).astype(F32).astype(BF16)
    out = out_ref[...].astype(BF16)
    weight = jnp.dot(out[:, :n_train], spread_train, preferred_element_type=F32)
    weight = weight * jnp.dot(out[:, n_train:], spread_query, preferred_element_type=F32)
    terms_ref[...] = jnp.sum(acc[...] * weight, axis=0, keepdims=True)


def make_shards(count, d_in, d_out):
    def shards(train_in, train_out, query_in, query_out, basis_in, basis_out, eigvals):
        me = lax.axis_index("blk").astype(jnp.int32).reshape(1)
        local = train_in.shape[0]
        queries = query_in.shape[0]
        width = basis_in.shape[0]
        rows = basis_out.shape[0]
        n_train = local * count
        bits = stage_bits(count)
        order = slot_order(count)
        chunk = width if width % 128 == 0 else 256
        chunks = order if width % 128 == 0 else [Fixed(k) for k in range(d_in // chunk)]
        early = min(2, len(chunks) - 1)
        block = 112 if rows % 112 == 0 else rows
        blocks = rows // block
        pieces = max(1, len(bits) - 1)
        cuts = [-(-k * blocks // pieces) for k in range(pieces + 1)]
        params = pltpu.CompilerParams(vmem_limit_bytes=20 * 2**20)
        eig_far = pltpu.with_memory_space_constraint(eigvals, pltpu.HBM)
        basis_far = pltpu.with_memory_space_constraint(basis_out, pltpu.HBM)

        def eig_sum(index, after, before):
            return pl.pallas_call(
                sum_kernel,
                grid=(cuts[index + 1] - cuts[index],),
                out_shape=jax.ShapeDtypeStruct((8, 128), F32),
                in_specs=[
                    whole(pl.ANY),
                    pl.BlockSpec((8, 128), lambda i: (0, 0)),
                    pl.BlockSpec((block, d_in), lambda i: (cuts[index] + i, 0)),
                ],
                out_specs=pl.BlockSpec((8, 128), lambda i: (0, 0)),
                compiler_params=params,
                cost_estimate=pl.CostEstimate(flops=rows * d_in // 4, bytes_accessed=rows * d_in, transcendentals=0),
                name="eig_sum",
            )(after, before, eig_far)

        stretch = 128
        stretches = d_out // stretch
        turns = min(len(bits), 4)
        out_cuts = [k * stretches // turns * stretch for k in range(turns + 1)]
        parts = 8 if rows % 128 == 0 else 1

        def held_shape(index):
            return jax.ShapeDtypeStruct((rows, out_cuts[index + 1] - out_cuts[index]), BF16)

        def load_first(after):
            return pl.pallas_call(
                lambda *refs: load_kernel(0, *refs),
                out_shape=held_shape(0),
                in_specs=[whole(pl.ANY), whole(pltpu.HBM)],
                out_specs=whole(),
                scratch_shapes=[pltpu.SemaphoreType.DMA((parts,))],
                compiler_params=params,
                cost_estimate=pl.CostEstimate(flops=0, bytes_accessed=rows * d_out // 2, transcendentals=0),
                name="load",
            )(after, basis_far)

        def rotate_out(index, after, before, stacked, held):
            out = jax.ShapeDtypeStruct((rows, n_train + queries), F32)
            cost = pl.CostEstimate(
                flops=rows * d_out * (n_train + queries) // 2, bytes_accessed=rows * d_out // 2, transcendentals=0
            )
            if index + 1 < turns:
                return pl.pallas_call(
                    lambda *refs: out_kernel(out_cuts[index], *refs),
                    out_shape=(out, held_shape(index + 1)),
                    in_specs=[whole(pl.ANY)] + [whole()] * 3 + [whole(pltpu.HBM)],
                    out_specs=(whole(), whole()),
                    scratch_shapes=[pltpu.SemaphoreType.DMA((parts,))],
                    compiler_params=params,
                    cost_estimate=cost,
                    name="rotate_out",
                )(after, before, stacked, held, basis_far)
            return pl.pallas_call(
                lambda *refs: last_out_kernel(out_cuts[index], chunks[:early], *refs),
                out_shape=(out, jax.ShapeDtypeStruct((early, rows, chunk), F32)),
                in_specs=[whole(SMEM), whole(pl.ANY)] + [whole()] * 3 + [whole(pltpu.HBM)],
                out_specs=(whole(), whole()),
                scratch_shapes=[pltpu.SemaphoreType.DMA((early,))],
                compiler_params=params,
                cost_estimate=cost,
                name="rotate_out_last",
            )(me, after, before, stacked, held, eig_far)

        def join(after, near, far, other=None):
            return pl.pallas_call(
                join_kernel,
                out_shape=jax.ShapeDtypeStruct((2 * near.shape[0],) + near.shape[1:], near.dtype),
                in_specs=[whole(pl.ANY), whole(pl.ANY), whole(), whole()],
                out_specs=whole(),
                compiler_params=params,
                name="join",
            )(after, after if other is None else other, near, far)

        held = pl.pallas_call(
            lambda *refs: pack_kernel(d_in, *refs),
            out_shape=jax.ShapeDtypeStruct((local, d_in + d_out), BF16),
            in_specs=[whole(pltpu.HBM)] * 2,
            out_specs=whole(),
            scratch_shapes=[pltpu.SemaphoreType.DMA((2,))],
            compiler_params=params,
            name="pack",
        )(pltpu.with_memory_space_constraint(train_in, pltpu.HBM), pltpu.with_memory_space_constraint(train_out, pltpu.HBM))
        total = jnp.zeros((8, 128), F32)
        query_part = None
        after = me
        for k, bit in enumerate(bits):
            got = swap(held, bit, count)
            if k == min(2, len(bits) - 1):
                query_part = pl.pallas_call(
                    query_kernel,
                    out_shape=jax.ShapeDtypeStruct((queries, width), BF16),
                    in_specs=[whole(pl.ANY), whole(), whole()],
                    out_specs=whole(),
                    compiler_params=params,
                    name="query_in",
                )(after, query_in, basis_in)
            if k < pieces and cuts[k] < cuts[k + 1]:
                total = eig_sum(k, after, total)
            after = got
            if k < len(bits) - 1:
                held = join(total, held, got, query_part)
        near, far = held, got
        basis_held = load_first(held)
        merged = pl.pallas_call(
            lambda *refs: train_kernel(count, local, d_in, *refs),
            out_shape=jax.ShapeDtypeStruct((n_train + queries + SUM_ROWS, width), BF16),
            in_specs=[whole(SMEM)] + [whole()] * 5,
            out_specs=whole(),
            compiler_params=params,
            name="train_in",
        )(me, near, far, basis_in, query_part, total)
        stacked = pl.pallas_call(
            lambda *refs: stack_kernel(d_in, *refs),
            out_shape=jax.ShapeDtypeStruct((n_train + queries, d_out), BF16),
            in_specs=[whole()] * 3,
            out_specs=whole(),
            compiler_params=params,
            name="stack",
        )(near, far, query_out)
        held = merged[None]
        after = merged
        out_part = jnp.zeros((rows, n_train + queries), F32)
        for k, bit in enumerate(bits):
            got = swap(held, bit, count)
            if k < turns:
                out_part, basis_held = rotate_out(k, after, out_part, stacked, basis_held)
            after = got
            if k < len(bits) - 1:
                held = join(out_part, held, got)
        near, far = held, got
        sums = (near, far)
        if isinstance(chunks[0], Fixed):
            back = jnp.argsort(jnp.asarray(order, jnp.int32))[me[0] ^ jnp.arange(count)]
            flat = jnp.take(jnp.concatenate([near, far], axis=0), back, axis=0).transpose(1, 0, 2)
            flat = flat.reshape(flat.shape[0], len(chunks), chunk).transpose(1, 0, 2)
            near, far = flat[: len(chunks) // 2], flat[len(chunks) // 2 :]
        terms = pl.pallas_call(
            lambda *refs: main_kernel(count, local, queries, 0.1 / (d_out * d_in), chunks, 4, *refs),
            out_shape=jax.ShapeDtypeStruct((1, n_train * queries), F32),
            in_specs=[whole(SMEM)] + [whole()] * 4 + [whole(pltpu.HBM), whole(), whole()],
            out_specs=whole(),
            scratch_shapes=[
                pltpu.VMEM((rows, n_train * queries), F32),
                pltpu.VMEM((len(chunks) - early, rows, chunk), F32),
                pltpu.SemaphoreType.DMA((len(chunks) - early,)),
            ],
            compiler_params=params,
            name="scores",
        )(me, *sums, near, far, eig_far, basis_held, out_part)
        return scatter_slots(terms.reshape(n_train, queries), count)

    return shards


def solution(mesh):
    in_specs = (
        P(("groups", "blk"), None),
        P(("groups", "blk"), None),
        P("groups", None),
        P("groups", None),
        P(("groups", "blk"), None),
        P(("groups", "blk"), None),
        P(("groups", "blk"), None),
    )
    out_specs = P(("groups", "blk"), None)
    count = mesh.shape["blk"]

    def run(train_in, train_out, query_in, query_out, basis_in, basis_out, eigvals):
        shards = make_shards(count, train_in.shape[1], train_out.shape[1])
        return jax.shard_map(shards, mesh=mesh, in_specs=in_specs, out_specs=out_specs, check_vma=False)(
            train_in, train_out, query_in, query_out, basis_in, basis_out, eigvals
        )

    return run
```
